256 devices in a mesh: zero: 16 (over z_hi, y, core), seq: 16 (over x, z_lo).
Axes of the slice: x: 4, y: 4, z: 8 (z_hi: 2, z_lo: 4; z = z_hi * 4 + z_lo), core: 2. Of those that a mesh axis runs over, the one named last changes fastest.
Arguments:
- features: bfloat16 [16, 8192, 1536], P('zero', 'seq'), may hold values from -12 to 12, as said below
- lengths: int32 [16], replicated, may hold values from 512 to 8192, as said below
- kernel: bfloat16 [31, 1536], P(None, 'zero'), may hold values from -1 to 1
- gain: bfloat16 [1536], P('zero'), may hold values from 0.5 to 1.5
- bias: bfloat16 [1536], P('zero'), may hold values from -3 to 3
- projection: bfloat16 [1536, 1536], P('zero'), may hold values from -0.15625 to 0.15625
- cotangent: bfloat16 [16, 8192, 1536], P('zero', 'seq'), may hold values from -6 to 6
Outputs:
- layer_out: bfloat16 [16, 8192, 1536], P('zero', 'seq')
- grad_features: bfloat16 [16, 8192, 1536], P('zero', 'seq')
- grad_projection: bfloat16 [1536, 1536], P('zero')
- grad_kernel: bfloat16 [31, 1536], P(None, 'zero')
- grad_gain: float32 [1536], P('zero')
- grad_bias: float32 [1536], P('zero')
The draws below stay inside these ranges and needn't reach their ends.
Inputs may be any that keep to these rules, and one draw needn't show every extreme that they name: `features`: input values; channels carry offsets that differ along the frames. `lengths`: at least one utterance has exactly 8192 valid frames.
All inputs are finite; a program needn't handle non-finite values.
Results may differ from the reference program's by a relative error of at most 0.0049.
Values may be sent and summed in bfloat16 or wider, within the bound.
A program may use at most 128 MiB of HBM per device.

```python
import jax
import jax.numpy as jnp
from jax import lax

D = 1536
K = 31
B = 16
L = 8192


def draw_features(key, part):
    key = jax.random.fold_in(key, 11)
    first_key, second_key = jax.random.split(key, 2)
    ramp = 1.0 + 2.0 * jnp.arange(L, dtype=jnp.float32) / L
    noise = jax.random.truncated_normal(first_key, -4.0, 4.0, (B, L, D), jnp.float32)
    offset = jax.random.uniform(second_key, (D,), jnp.float32, -1.5, 1.5)
    return (noise + offset[None, None, :] * ramp[None, :, None]).astype(jnp.bfloat16)


def draw_lengths(key, part):
    key = jax.random.fold_in(key, 23)
    first_key, second_key = jax.random.split(key)
    chosen = jax.random.randint(first_key, (), 0, B)
    others = jax.random.randint(second_key, (B,), L // 16, 5 * L // 8)
    return jnp.where(jnp.arange(B, dtype=jnp.int32) == chosen, L, others).astype(jnp.int32)


def draw_cotangent(key, part):
    key = jax.random.fold_in(key, 37)
    first_key, second_key = jax.random.split(key)
    noise = jax.random.truncated_normal(first_key, -4.0, 4.0, (B, L, D), jnp.float32)
    offset = jax.random.uniform(second_key, (D,), jnp.float32, -0.35, 0.35)
    return jnp.clip(noise + offset[None, None, :], -6.0, 6.0).astype(jnp.bfloat16)


def level_of(key, dims, cuts, low, top_value):
    def one(position, parts):
        steps = jax.random.uniform(jax.random.fold_in(jax.random.fold_in(key, 6), position), (parts,), jnp.float32, low / len(cuts), top_value / len(cuts))
        return jnp.repeat(jnp.exp(steps), dims[position] // parts).reshape((-1,) + (1,) * (len(dims) - position - 1))

    level = one(*cuts[0])
    for cut in cuts[1:]:
        level = level * one(*cut)
    return level


def bell_draw(stream_key, extent, scale, bound, pieces=(), kind=jnp.bfloat16):
    result = scale * jax.random.normal(stream_key, extent, jnp.float32)
    if pieces:
        result = result * level_of(stream_key, extent, pieces, -0.22, 0.18)
    return jnp.clip(result, -bound, bound).astype(kind)


def setup_inputs(seed: int = 0) -> dict:
    arg_keys = jax.random.split(jax.random.key(seed), 8)
    return {
        "features": draw_features(jax.random.fold_in(arg_keys[7], 71), 0),
        "lengths": draw_lengths(jax.random.fold_in(arg_keys[7], 71), 0),
        "kernel": bell_draw(arg_keys[2], (K, D), K ** -0.5, 1.0, ((1, 16),)),
        "gain": jnp.clip(0.5 + 1.0 * jax.random.uniform(arg_keys[3], (D,), jnp.float32) ** level_of(arg_keys[3], (D,), ((0, 16),), -0.2, 0.2), 0.5, 1.5).astype(jnp.bfloat16),
        "bias": bell_draw(arg_keys[4], (D,), 0.5, 3.0, ((0, 16),)),
        "projection": bell_draw(arg_keys[5], (D, D), D ** -0.5, 0.15625, ((0, 16),)),
        "cotangent": draw_cotangent(jax.random.fold_in(arg_keys[7], 71), 0),
    }


EPS = 1e-05

def conv_pieces(frames, keep, kernel):
    reach = kernel.shape[0] // 2
    inputs = frames.astype(jnp.float32) * keep
    padded = jnp.pad(inputs, ((reach, reach), (0, 0)))
    length = inputs.shape[0]
    total = jnp.zeros(inputs.shape, jnp.float32)
    for shift in range(kernel.shape[0]):
        total = total + kernel[shift].astype(jnp.float32)[None, :] * padded[shift:shift + length]
    return (total, padded)

def reference(features, lengths, kernel, gain, bias, projection, cotangent):
    positions = jnp.arange(features.shape[1], dtype=jnp.int32)
    masks = (positions[None, :] < lengths[:, None]).astype(jnp.float32)[:, :, None]
    count = jnp.sum(lengths).astype(jnp.float32)
    scale_g = gain.astype(jnp.float32)
    shift_b = bias.astype(jnp.float32)
    width = features.shape[2]
    reach = kernel.shape[0] // 2
    zeros_d = jnp.zeros((width,), jnp.float32)

    def first(carry, item):
        frames, keep = item
        conv, _ = conv_pieces(frames, keep, kernel)
        return (carry + lax.optimization_barrier(jnp.sum(conv * keep, axis=0)), None)
    total, _ = lax.scan(first, zeros_d, (features, masks))
    mean = total / count

    def second(carry, item):
        frames, keep = item
        conv, _ = conv_pieces(frames, keep, kernel)
        deviation = (conv - mean) * keep
        return (carry + lax.optimization_barrier(jnp.sum(deviation * deviation, axis=0)), None)
    squares, _ = lax.scan(second, zeros_d, (features, masks))
    rstd = lax.rsqrt(squares / count + EPS)

    def forward(carry, item):
        weight_sum, bias_sum, gain_sum = carry
        frames, keep, upstream = item
        conv, _ = conv_pieces(frames, keep, kernel)
        normed = (conv - mean) * rstd
        pre = normed * scale_g + shift_b
        sig = jax.nn.sigmoid(pre)
        hidden = (keep * pre * sig).astype(jnp.bfloat16)
        output = jnp.dot(hidden, projection, preferred_element_type=jnp.float32).astype(jnp.bfloat16)
        back = lax.dot_general(upstream, projection, (((1,), (1,)), ((), ())), preferred_element_type=jnp.float32)
        dpre = keep * back * (sig * (1.0 + pre * (1.0 - sig)))
        weight_sum = weight_sum + lax.dot_general(hidden, upstream, (((0,), (0,)), ((), ())), preferred_element_type=jnp.float32)
        bias_sum = bias_sum + lax.optimization_barrier(jnp.sum(dpre, axis=0))
        gain_sum = gain_sum + lax.optimization_barrier(jnp.sum(dpre * normed, axis=0))
        return ((weight_sum, bias_sum, gain_sum), (output, dpre))
    start = (jnp.zeros((width, width), jnp.float32), zeros_d, zeros_d)
    (weight_sum, bias_sum, gain_sum), (outputs, dpres) = lax.scan(forward, start, (features, masks, cotangent))

    def backward(carry, item):
        frames, keep, dpre = item
        conv, padded = conv_pieces(frames, keep, kernel)
        length = conv.shape[0]
        normed = (conv - mean) * rstd
        dconv = keep * rstd * scale_g * (dpre - bias_sum / count - normed * gain_sum / count)
        dpad = jnp.pad(dconv, ((reach, reach), (0, 0)))
        dframes = jnp.zeros(conv.shape, jnp.float32)
        rows = []
        for shift in range(kernel.shape[0]):
            dframes = dframes + kernel[shift].astype(jnp.float32)[None, :] * dpad[2 * reach - shift:2 * reach - shift + length]
            rows.append(lax.optimization_barrier(jnp.sum(dconv * padded[shift:shift + length], axis=0)))
        grad_frames = (keep * dframes).astype(jnp.bfloat16)
        return (carry + jnp.stack(rows, axis=0), grad_frames)
    kernel_sum, grad_features = lax.scan(backward, jnp.zeros(kernel.shape, jnp.float32), (features, masks, dpres))
    root = lax.rsqrt(count)
    return (outputs, grad_features, (weight_sum * root).astype(jnp.bfloat16), (kernel_sum * root).astype(jnp.bfloat16), gain_sum * root, bias_sum * root)
```

```python
import functools

import jax
import jax.numpy as jnp
from jax import lax
from jax.experimental import pallas as pl
from jax.experimental.pallas import tpu as pltpu
from jax.sharding import PartitionSpec as P

EPS = 1e-05
LANES = 128
HALO = 16
MESH = pl.DeviceIdType.MESH
F32 = jnp.float32
BF16 = jnp.bfloat16


class Dims:
    def __init__(self, zero, seq, frames, width, taps):
        self.nc = 2
        self.nzh = 2
        self.ny = zero // 4
        self.nx = 2 if seq == 4 else 4
        self.nzl = seq // self.nx
        self.zero, self.seq = zero, seq
        self.f, self.d, self.k = frames, width, taps
        self.nt = width // LANES
        self.blk = width // zero
        self.ext = frames + 2 * HALO
        self.chunk = min(128, frames)
        self.q = self.ny * self.nzh
        self.half = self.blk // 2
        self.cols = width // self.nx
        self.piece = self.blk // self.nzl
        self.pad_piece = -(-self.piece // 16) * 16
        self.sub = self.nzl // 2
        self.win = 4 * self.blk // LANES
        self.krows = -(-(taps + 2) // 8) * 8
        self.srows = -(-(taps + 2) // 16) * 16


def fold(values):
    rows = values.shape[0]
    return jnp.sum(values.reshape(rows // 8, 8, LANES), axis=0)


def kernel(
    g, sc, feat, cot, proj, small, keep,
    out, gfeat, gproj, gsmall,
    x_s, cv, dp, tap, full, hid, hid_t, ht2, cot_sib, halo, sm,
    a1, b1, a2, b2, st1, st2, gacc, gfull, gsend, ga, gb,
    wf, ws, r1x, r1y, s0, s1, r2x, r2y, tt, r3, wfin, asm,
    ssem, rsem, halo_s, halo_r, hal2_s, hal2_r, cot_s, cot_r, pj_s, pj_r, ht_s, ht_r,
    p1_s, p1_r, p2_s, p2_r, p3_s, p3_r,
):
    zi = lax.axis_index("zero")
    si = lax.axis_index("seq")
    c = zi % g.nc
    y = (zi // g.nc) % g.ny
    zh = zi // (g.nc * g.ny)
    zl = si % g.nzl
    x = si // g.nzl

    def zero_of(h, yy, cc):
        return (h * g.ny + yy) * g.nc + cc

    def seq_of(xx, zz):
        return xx * g.nzl + zz

    sibling = (zero_of(zh, y, 1 - c), si)

    def remote(src, dst, ss, rs, device):
        return pltpu.make_async_remote_copy(
            src_ref=src, dst_ref=dst, send_sem=ss, recv_sem=rs,
            device_id=device, device_id_type=MESH,
        )

    def in_zero(peer):
        return (peer, si)

    def in_seq(peer):
        return (zi, peer)

    def spread(buf, e, me, n, dev):
        @pl.loop(1, n)
        def _(o):
            peer = (me + o) % n
            remote(buf.at[me], buf.at[me], ssem.at[e, o], rsem.at[e, me], dev(peer)).start()

    def gathered(buf, e, me, n, dev):
        @pl.loop(1, n)
        def _(o):
            peer = (me + n - o) % n
            remote(buf.at[peer], buf.at[peer], ssem.at[e, o], rsem.at[e, peer], dev(peer)).wait()

    barrier = pltpu.get_barrier_semaphore()

    @pl.loop(1, g.zero)
    def _(o):
        pl.semaphore_signal(barrier, inc=1, device_id=((zi + o) % g.zero, si), device_id_type=MESH)

    @pl.loop(1, g.seq)
    def _(o):
        pl.semaphore_signal(barrier, inc=1, device_id=(zi, (si + o) % g.seq), device_id_type=MESH)

    @pl.loop(1, g.nzl)
    def _(o):
        pl.semaphore_signal(
            barrier, inc=1,
            device_id=(zero_of(1 - zh, y, c), seq_of(x, (zl + o) % g.nzl)), device_id_type=MESH,
        )

    @pl.loop(0, g.nt)
    def _(l):
        lane = pl.ds(pl.multiple_of(l * LANES, LANES), LANES)
        x_s[l, HALO:HALO + g.f, :] = feat[:, lane].astype(F32) * keep[HALO:HALO + g.f, :]

    own_rows = pl.ds(pl.multiple_of(zi * g.blk, 16), g.blk)
    full[own_rows, :] = proj[...]
    sm[zi] = small[...]
    pl.semaphore_wait(barrier, g.zero - 1 + g.seq - 1 + g.nzl - 1)

    spread(sm, 0, zi, g.zero, in_zero)
    right = in_seq((si + 1) % g.seq)
    left = in_seq((si + g.seq - 1) % g.seq)
    halo_right = remote(feat.at[pl.ds(g.f - HALO, HALO)], halo.at[0], halo_s.at[0], halo_r.at[0], right)
    halo_left = remote(feat.at[pl.ds(0, HALO)], halo.at[1], halo_s.at[1], halo_r.at[1], left)
    halo_right.start()
    halo_left.start()

    def block(index):
        return full.at[pl.ds(pl.multiple_of(index * g.blk, 16), g.blk)]

    def send_block(index, slot, device):
        remote(block(index), block(index), pj_s.at[slot], pj_r.at[index], device).start()

    def wait_block(index):
        remote(block(index), block(index), pj_s.at[0], pj_r.at[index], sibling).wait_recv()

    other = zero_of(1 - zh, y, c)
    mirror = (other, seq_of(x, g.nzl - 1 - zl))
    send_block(zi, 0, mirror)

    @pl.loop(1, g.ny)
    def _(o):
        send_block(zi, o, in_zero(zero_of(zh, (y + o) % g.ny, c)))

    cot_copy = remote(cot, cot_sib, cot_s, cot_r, sibling)
    send_block(zi, g.ny, sibling)
    cot_copy.start()

    gathered(sm, 0, zi, g.zero, in_zero)
    for w in range(g.zero // 4):
        total = None
        for i in range(4):
            row = lax.broadcasted_iota(jnp.int32, (LANES, 4 * g.blk), 0)
            col = lax.broadcasted_iota(jnp.int32, (LANES, 4 * g.blk), 1)
            place = jnp.where((col == row + i * g.blk) & (row < g.blk), 1.0, 0.0).astype(BF16)
            term = jnp.dot(sm[4 * w + i], place, preferred_element_type=F32)
            total = term if total is None else total + term
        for j in range(g.win):
            tap[g.win * w + j] = total[:, j * LANES:(j + 1) * LANES]
    halo_right.wait()
    halo_left.wait()

    @pl.loop(0, g.nt)
    def _(l):
        lane = pl.ds(pl.multiple_of(l * LANES, LANES), LANES)
        x_s[l, 0:HALO, :] = halo[0, :, lane].astype(F32) * keep[0:HALO, :]
        x_s[l, HALO + g.f:, :] = halo[1, :, lane].astype(F32) * keep[HALO + g.f:, :]

    own_keep = keep.at[pl.ds(HALO, g.f)]

    def conv_tiles(first, last):
        @pl.loop(first, last)
        def _(l):
            acc = jnp.zeros((g.f, LANES), F32)
            for k in range(g.k):
                acc = acc + tap[l, k:k + 1, :] * x_s[l, k + 1:k + 1 + g.f, :]
            cv[l, HALO:HALO + g.f, :] = acc
            mask = own_keep[...]
            mean = jnp.sum(fold(acc * mask), axis=0, keepdims=True) * sc[32]
            dev = (cv[l, HALO:HALO + g.f, :] - mean) * mask
            a1[zi, pl.ds(l, 1), :] = mean
            a1[zi, pl.ds(g.nt + l, 1), :] = jnp.sum(fold(dev * dev), axis=0, keepdims=True)

    def pooled(buf, n, base, inverse):
        total = None
        for i in range(n):
            term = sc[base + i] * buf[i, 0:g.nt, :]
            total = term if total is None else total + term
        mean = total * inverse
        squares = None
        for i in range(n):
            dev = buf[i, 0:g.nt, :] - mean
            term = buf[i, g.nt:2 * g.nt, :] + sc[base + i] * (dev * dev)
            squares = term if squares is None else squares + term
        return mean, squares

    conv_tiles(0, g.nt // 2)
    wait_block(other)
    send_block(other, g.ny + 1, sibling)

    @pl.loop(1, g.ny)
    def _(o):
        send_block(other, g.ny + 1 + o, in_zero(zero_of(zh, (y + o) % g.ny, c)))

    @pl.loop(1, g.ny)
    def _(o):
        index = zero_of(zh, (y + o) % g.ny, c)
        wait_block(index)
        send_block(index, 2 * g.ny + o, sibling)

    conv_tiles(g.nt // 2, g.nt)
    spread(a1, 1, zi, g.zero, in_zero)
    gathered(a1, 1, zi, g.zero, in_zero)
    mean_a, squares_a = pooled(a1, g.zero, 0, sc[33])
    b1[si, 0:g.nt, :] = mean_a
    b1[si, g.nt:2 * g.nt, :] = squares_a
    spread(b1, 2, si, g.seq, in_seq)

    @pl.loop(1, g.ny)
    def _(o):
        index = zero_of(1 - zh, (y + o) % g.ny, c)
        wait_block(index)
        send_block(index, 3 * g.ny - 1 + o, sibling)

    @pl.loop(0, g.nzh * g.ny)
    def _(j):
        wait_block(j * g.nc + 1 - c)

    @pl.loop(0, 4 * g.ny - 1)
    def _(slot):
        remote(block(zi), block(zi), pj_s.at[slot], pj_r.at[0], sibling).wait_send()

    @pl.loop(0, g.nt // 2)
    def _(n):
        rows = pl.ds(pl.multiple_of(n * 256, 256), 256)
        back = lax.dot_general(
            cot[...], full[rows, :], (((1,), (1,)), ((), ())), preferred_element_type=F32
        )
        dp[2 * n, HALO:HALO + g.f, :] = back[:, :LANES]
        dp[2 * n + 1, HALO:HALO + g.f, :] = back[:, LANES:]

    gathered(b1, 2, si, g.seq, in_seq)
    mean, squares = pooled(b1, g.seq, 16, sc[34])
    st1[0:g.nt, :] = mean
    st1[g.nt:2 * g.nt, :] = lax.rsqrt(squares * sc[34] + EPS)

    @pl.loop(0, g.nt)
    def _(l):
        lane = pl.ds(pl.multiple_of(l * LANES, LANES), LANES)
        mean_l = st1[pl.ds(l, 1), :]
        rstd_l = st1[pl.ds(g.nt + l, 1), :]
        gain_l = tap[l, g.k:g.k + 1, :]
        bias_l = tap[l, g.k + 1:g.k + 2, :]

        def step(r, sums):
            bias_sum, gain_sum = sums
            base = pl.multiple_of(r * g.chunk, g.chunk)
            rows = pl.ds(base + HALO, g.chunk)
            mask = keep[rows, :]
            normed = (cv[l, rows, :] - mean_l) * rstd_l
            cv[l, rows, :] = normed
            pre = normed * gain_l + bias_l
            sig = jax.nn.sigmoid(pre)
            hidden = mask * pre * sig
            hid[pl.ds(base, g.chunk), lane] = hidden.astype(BF16)
            hid_t[lane, pl.ds(base, g.chunk)] = hidden.T.astype(BF16)
            dpre = mask * dp[l, rows, :] * (sig * (1.0 + pre * (1.0 - sig)))
            dp[l, rows, :] = dpre
            return bias_sum + fold(dpre), gain_sum + fold(dpre * normed)

        zero = jnp.zeros((8, LANES), F32)
        bias_sum, gain_sum = lax.fori_loop(0, g.f // g.chunk, step, (zero, zero))
        a2[zi, pl.ds(l, 1), :] = jnp.sum(bias_sum, axis=0, keepdims=True)
        a2[zi, pl.ds(g.nt + l, 1), :] = jnp.sum(gain_sum, axis=0, keepdims=True)

    spread(a2, 3, zi, g.zero, in_zero)

    def hidden_rows(q, cc):
        return pl.ds(pl.multiple_of(zero_of(q % g.nzh, q // g.nzh, cc) * g.blk, 16), g.blk)

    def hidden_copy(q):
        return remote(
            hid_t.at[hidden_rows(q, 1 - c)],
            ht2.at[1, pl.ds(pl.multiple_of(q * g.blk, 16), g.blk)],
            ht_s.at[q], ht_r.at[q], sibling,
        )

    @pl.loop(0, g.q)
    def _(q):
        hidden_copy(q).start()

    edges = []
    for i, buf in enumerate((dp, cv)):
        edges.append(remote(
            buf.at[:, pl.ds(g.f, HALO), :], buf.at[:, pl.ds(0, HALO), :],
            hal2_s.at[2 * i], hal2_r.at[2 * i], right))
        edges.append(remote(
            buf.at[:, pl.ds(HALO, HALO), :], buf.at[:, pl.ds(g.f + HALO, HALO), :],
            hal2_s.at[2 * i + 1], hal2_r.at[2 * i + 1], left))
    for edge in edges:
        edge.start()

    @pl.loop(0, g.q)
    def _(q):
        ht2[0, pl.ds(pl.multiple_of(q * g.blk, 16), g.blk), :] = hid_t[hidden_rows(q, c), :]

    gathered(a2, 3, zi, g.zero, in_zero)
    total = a2[0]
    for i in range(1, g.zero):
        total = total + a2[i]
    b2[si] = total
    spread(b2, 4, si, g.seq, in_seq)

    cot_copy.wait()

    @pl.loop(0, g.q)
    def _(q):
        hidden_copy(q).wait()

    def part0_copy(o, target, sender):
        return remote(
            ws.at[0, :, :, target], r1x.at[sender], p1_s.at[0, o], p1_r.at[0, sender],
            in_seq(seq_of(target, zl)),
        )

    def part1_copy(o, target, sender):
        return remote(
            ws.at[1, target], r1y.at[sender], p1_s.at[1, o], p1_r.at[1, sender],
            in_zero(zero_of(zh, target, c)),
        )

    @pl.loop(1, g.nx + 1)
    def _(o):
        xx = (x + o) % g.nx
        col = pl.ds(pl.multiple_of(xx * g.cols, LANES), g.cols)
        wf[...] = jnp.dot(ht2[0], cot[:, col], preferred_element_type=F32) + jnp.dot(
            ht2[1], cot_sib[:, col], preferred_element_type=F32
        )
        for yy in range(g.ny):
            for hh in range(g.nzh):
                row = (yy * g.nzh + hh) * g.blk
                ws[0, yy, hh, xx] = wf[row:row + g.half, :].astype(BF16)
                ws[1, yy, hh, xx] = wf[row + g.half:row + g.blk, :].astype(BF16)
        for hh in range(g.nzh):
            row = pl.multiple_of((y * g.nzh + hh) * g.blk + g.half, 8)
            s1[hh, xx] = wf[pl.ds(row, g.half), :]

        @pl.when(o < g.nx)
        def _():
            part0_copy(o, xx, x).start()

    for yy in range(g.ny):
        for hh in range(g.nzh):
            row = (yy * g.nzh + hh) * g.blk
            s0[yy, hh] = wf[row:row + g.half, :]

    @pl.loop(1, g.ny)
    def _(o):
        part1_copy(o, (y + o) % g.ny, y).start()

    @pl.loop(0, g.nt // 2)
    def _(n):
        col = pl.ds(pl.multiple_of(n * 256, 256), 256)
        out[:, col] = jnp.dot(hid[...], full[:, col], preferred_element_type=F32).astype(BF16)

    gathered(b2, 4, si, g.seq, in_seq)
    total = b2[0]
    for i in range(1, g.seq):
        total = total + b2[i]
    st2[...] = total * sc[34]
    for edge in edges:
        edge.wait()

    def backward_tiles(first, last):
        @pl.loop(first, last)
        def _(l):
            lane = pl.ds(pl.multiple_of(l * LANES, LANES), LANES)
            scale = st1[pl.ds(g.nt + l, 1), :] * tap[l, g.k:g.k + 1, :]
            bias_m = st2[pl.ds(l, 1), :]
            gain_m = st2[pl.ds(g.nt + l, 1), :]
            dp[l] = keep[...] * scale * (dp[l] - bias_m - cv[l] * gain_m)
            gacc[...] = jnp.zeros(gacc.shape, F32)

            @pl.loop(0, g.f // g.chunk)
            def _(r):
                base = pl.multiple_of(r * g.chunk, g.chunk)
                here = dp[l, pl.ds(base + HALO, g.chunk), :]
                acc = jnp.zeros((g.chunk, LANES), F32)
                for k in range(g.k):
                    gacc[k] = gacc[k] + fold(here * x_s[l, pl.ds(base + k + 1, g.chunk), :])
                    acc = acc + tap[l, k:k + 1, :] * dp[l, pl.ds(base + 2 * HALO - 1 - k, g.chunk), :]
                mask = keep[pl.ds(base + HALO, g.chunk), :]
                gfeat[pl.ds(base, g.chunk), lane] = (mask * acc).astype(BF16)

            gfull[l, 0:32, :] = jnp.sum(gacc[...], axis=1)
            gfull[l, 32:g.krows, :] = jnp.zeros((g.krows - 32, LANES), F32)
            gfull[l, g.k:g.k + 1, :] = a2[zi, pl.ds(l, 1), :]
            gfull[l, g.k + 1:g.k + 2, :] = a2[zi, pl.ds(g.nt + l, 1), :]

    def second0_copy(o, target, sender):
        return remote(
            s0.at[target], r2y.at[sender], p2_s.at[0, o], p2_r.at[0, sender],
            in_zero(zero_of(zh, target, c)),
        )

    def second1_copy(o, target, sender):
        return remote(
            s1.at[:, target], r2x.at[sender], p2_s.at[1, o], p2_r.at[1, sender],
            in_seq(seq_of(target, zl)),
        )

    def third_copy(o):
        me = zh * g.nzl + zl
        peer = (me + o) % (g.nzh * g.nzl)
        hh, zz = peer // g.nzl, peer % g.nzl
        row = pl.ds(pl.multiple_of((zz % g.sub) * g.piece, 8), g.piece)
        return remote(
            tt.at[zz // g.sub, hh, row], r3.at[me], p3_s.at[o], p3_r.at[me],
            (zero_of(hh, y, c), seq_of(x, zz)),
        )

    def third_wait(o):
        me = zh * g.nzl + zl
        peer = (me + g.nzh * g.nzl - o) % (g.nzh * g.nzl)
        remote(r3.at[peer], r3.at[peer], p3_s.at[o], p3_r.at[peer], sibling).wait()

    backward_tiles(0, g.nt // 2)

    @pl.loop(1, g.nx)
    def _(o):
        part0_copy(o, x, (x + g.nx - o) % g.nx).wait()

    @pl.loop(1, g.ny)
    def _(o):
        part1_copy(o, y, (y + g.ny - o) % g.ny).wait()

    @pl.loop(1, g.nx)
    def _(o):
        s0[...] = s0[...] + r1x[(x + o) % g.nx].astype(F32)

    @pl.loop(1, g.ny)
    def _(o):
        s1[...] = s1[...] + r1y[(y + o) % g.ny].astype(F32)

    @pl.loop(1, g.ny)
    def _(o):
        second0_copy(o, (y + o) % g.ny, y).start()

    @pl.loop(1, g.nx)
    def _(o):
        second1_copy(o, (x + o) % g.nx, x).start()

    backward_tiles(g.nt // 2, g.nt)

    @pl.loop(1, g.ny)
    def _(o):
        second0_copy(o, y, (y + g.ny - o) % g.ny).wait()

    @pl.loop(1, g.nx)
    def _(o):
        second1_copy(o, x, (x + g.nx - o) % g.nx).wait()

    first = s0[y]
    second = s1[:, x]
    for o in range(1, g.ny):
        first = first + r2y[(y + o) % g.ny]
    for o in range(1, g.nx):
        second = second + r2x[(x + o) % g.nx]
    tt[0] = first
    tt[1] = second

    @pl.loop(1, g.nzh * g.nzl)
    def _(o):
        third_copy(o).start()

    lanes = lax.broadcasted_iota(jnp.int32, (g.krows, LANES), 1)
    for m in range(g.zero):
        t0, off = (m * g.blk) // LANES, (m * g.blk) % LANES
        value = gfull[t0]
        if off:
            value = pltpu.roll(value, LANES - off, 1)
            if off + g.blk > LANES:
                value = jnp.where(lanes < LANES - off, value, pltpu.roll(gfull[t0 + 1], LANES - off, 1))
        gsend[m] = value

    def owner_copy(o, target, sender):
        return remote(gsend.at[target], ga.at[sender], ssem.at[5, o], rsem.at[5, sender], in_zero(target))

    @pl.loop(1, g.zero)
    def _(o):
        owner_copy(o, (zi + o) % g.zero, zi).start()

    @pl.loop(1, g.nzh * g.nzl)
    def _(o):
        third_wait(o)

    mine = pl.ds(pl.multiple_of((zl % g.sub) * g.piece, 8), g.piece)
    r3[zh * g.nzl + zl] = tt[zl // g.sub, zh, mine, :]
    total = r3[0]
    for i in range(1, g.nzh * g.nzl):
        total = total + r3[i]
    if g.pad_piece > g.piece:
        total = jnp.concatenate([total, jnp.zeros((g.pad_piece - g.piece, g.cols), F32)], axis=0)
    wfin[si] = (total * sc[35]).astype(BF16)
    spread(wfin, 6, si, g.seq, in_seq)

    @pl.loop(1, g.zero)
    def _(o):
        owner_copy(o, zi, (zi + g.zero - o) % g.zero).wait()

    ga[zi] = gsend[zi]
    total = ga[0]
    for i in range(1, g.zero):
        total = total + ga[i]
    gb[si] = total
    spread(gb, 7, si, g.seq, in_seq)

    gathered(wfin, 6, si, g.seq, in_seq)
    for s in range(g.seq):
        row, col = (s % g.nzl) * g.piece, (s // g.nzl) * g.cols
        asm[row:row + g.piece, col:col + g.cols] = wfin[s].astype(F32)[0:g.piece]
    gproj[...] = asm[...].astype(BF16)

    gathered(gb, 7, si, g.seq, in_seq)
    total = gb[0]
    for i in range(1, g.seq):
        total = total + gb[i]
    gsmall[...] = total * sc[35]


def fused(g, *operands):
    vmem = pltpu.VMEM
    dma = pltpu.SemaphoreType.DMA
    planes = (g.nt, g.ext, LANES)
    stats = (2 * g.nt, LANES)
    scratch = [
        vmem(planes, F32),
        vmem(planes, F32),
        vmem(planes, F32),
        vmem((g.nt, g.srows, LANES), F32),
        vmem((g.d, g.d), BF16),
        vmem((g.f, g.d), BF16),
        vmem((g.d, g.f), BF16),
        vmem((2, g.q * g.blk, g.f), BF16),
        vmem((g.f, g.d), BF16),
        vmem((2, HALO, g.d), BF16),
        vmem((g.zero, g.srows, LANES), BF16),
        vmem((g.zero,) + stats, F32),
        vmem((g.seq,) + stats, F32),
        vmem((g.zero,) + stats, F32),
        vmem((g.seq,) + stats, F32),
        vmem(stats, F32),
        vmem(stats, F32),
        vmem((32, 8, LANES), F32),
        vmem((g.nt, g.krows, LANES), F32),
        vmem((g.zero, g.krows, LANES), F32),
        vmem((g.zero, g.krows, LANES), F32),
        vmem((g.seq, g.krows, LANES), F32),
        vmem((g.q * g.blk, g.cols), F32),
        vmem((2, g.ny, g.nzh, g.nx, g.half, g.cols), BF16),
        vmem((g.nx, g.ny, g.nzh, g.half, g.cols), BF16),
        vmem((g.ny, g.nzh, g.nx, g.half, g.cols), BF16),
        vmem((g.ny, g.nzh, g.half, g.cols), F32),
        vmem((g.nzh, g.nx, g.half, g.cols), F32),
        vmem((g.nx, g.nzh, g.half, g.cols), F32),
        vmem((g.ny, g.nzh, g.half, g.cols), F32),
        vmem((2, g.nzh, g.half, g.cols), F32),
        vmem((g.nzh * g.nzl, g.piece, g.cols), F32),
        vmem((g.seq, g.pad_piece, g.cols), BF16),
        vmem((g.blk, g.d), F32),
        dma((8, 16)), dma((8, 16)),
        dma((2,)), dma((2,)), dma((4,)), dma((4,)), dma, dma,
        dma((4 * g.ny,)), dma((g.zero,)), dma((g.q,)), dma((g.q,)),
        dma((2, 4)), dma((2, 4)), dma((2, 4)), dma((2, 4)),
        dma((g.nzh * g.nzl,)), dma((g.nzh * g.nzl,)),
    ]
    whole = pl.BlockSpec(memory_space=pltpu.VMEM)
    return pl.pallas_call(
        functools.partial(kernel, g),
        name="conformer_conv",
        out_shape=[
            jax.ShapeDtypeStruct((g.f, g.d), BF16),
            jax.ShapeDtypeStruct((g.f, g.d), BF16),
            jax.ShapeDtypeStruct((g.blk, g.d), BF16),
            jax.ShapeDtypeStruct((g.krows, LANES), F32),
        ],
        in_specs=[pl.BlockSpec(memory_space=pltpu.SMEM)] + [whole] * 5,
        out_specs=[whole] * 4,
        scratch_shapes=scratch,
        compiler_params=pltpu.CompilerParams(
            collective_id=0, has_side_effects=True, vmem_limit_bytes=56 * 1024 * 1024
        ),
    )(*operands)


def shards(features, lengths, kernel_taps, gain, bias, projection, cotangent):
    frames, width = features.shape[1:]
    taps = kernel_taps.shape[0]
    zero, seq = lax.axis_size("zero"), lax.axis_size("seq")
    g = Dims(zero, seq, frames, width, taps)
    member, place = lax.axis_index("zero"), lax.axis_index("seq")
    here = place * frames
    own_length = lengths[member]
    positions = here - HALO + jnp.arange(g.ext, dtype=jnp.int32)
    keep = ((positions >= 0) & (positions < own_length)).astype(F32)
    keep = jnp.broadcast_to(keep[:, None], (g.ext, LANES))
    spans = jnp.clip(lengths[:, None] - jnp.arange(seq, dtype=jnp.int32)[None, :] * frames, 0, frames)
    valid_a = lax.dynamic_index_in_dim(spans, place, axis=1, keepdims=False).astype(F32)
    valid_b = jnp.sum(spans, axis=0).astype(F32)
    count = jnp.sum(lengths).astype(F32)

    def inverse(n):
        return 1.0 / jnp.maximum(n, 1.0)

    scalars = jnp.concatenate([
        jnp.pad(valid_a, (0, 16 - zero)), jnp.pad(valid_b, (0, 16 - seq)),
        jnp.stack([
            inverse(valid_a[member]), inverse(valid_b[place]), 1.0 / count, lax.rsqrt(count),
        ]),
    ])
    small = jnp.concatenate([kernel_taps, gain[None, :], bias[None, :]], axis=0)
    small = jnp.pad(small, ((0, g.srows - small.shape[0]), (0, LANES - small.shape[1])))
    out, gfeat, gproj, gsmall = fused(
        g, scalars, features[0], cotangent[0], projection, small, keep
    )
    return (
        out[None], gfeat[None], gproj,
        gsmall[:taps, :g.blk].astype(BF16),
        gsmall[taps + 1, :g.blk],
        gsmall[taps, :g.blk],
    )


def solution(mesh):
    in_specs = (
        P("zero", "seq", None),
        P(),
        P(None, "zero"),
        P("zero"),
        P("zero"),
        P("zero", None),
        P("zero", "seq", None),
    )
    out_specs = (
        P("zero", "seq", None),
        P("zero", "seq", None),
        P("zero", None),
        P(None, "zero"),
        P("zero"),
        P("zero"),
    )
    return jax.shard_map(shards, mesh=mesh, in_specs=in_specs, out_specs=out_specs, check_vma=False)
```
